256 devices in a mesh: depth: 8 (over x_hi, y), lat: 32 (over z, x_lo, core).
Axes of the slice: x: 4 (x_hi: 2, x_lo: 2; x = x_hi * 2 + x_lo), y: 4, z: 8, core: 2. Of those that a mesh axis runs over, the one named last changes fastest.
Arguments:
- operator: float32 [8, 160, 9, 256, 128], P('depth', 'lat'), may hold values from -0.125 to 0.125
- band_shift: int32 [8, 160], P('depth', 'lat'), may hold values from -1 to 1, as said below
- reflectivity: float32 [8, 20480], P('depth', 'lat'), may hold values from -0.4 to 0.4
- up_stored: float32 [8, 20480, 128], P('depth', 'lat'), may hold values from -6 to 6
- down_stored: float32 [8, 20480, 128], P('depth', 'lat'), may hold values from -6 to 6
- sources: float32 [20480, 128], P('lat'), may hold values from -6 to 6
- assignment: int32 [64], replicated, may hold values from 0 to 63, each once
Outputs:
- down_fields: float32 [8, 20480, 128], P('depth', 'lat')
- up_fields: float32 [8, 20480, 128], P('depth', 'lat')
The draws below stay inside these ranges and needn't reach their ends.
Inputs may be any that keep to these rules, and one draw needn't show every extreme that they name: `band_shift`: in every section some tile row has -1 and some has +1.
All inputs are finite; a program needn't handle non-finite values.
Results may differ from the reference program's by a relative error of at most 0.00013.
Values sent between devices are 32-bit elements; how exact they have to be, the bound alone decides.
A program may use at most 64 MiB of HBM per device.

```python
import jax
import jax.numpy as jnp
from jax import lax

TILE = 128
SHOTS = 32
SECTIONS = 8
LAT_TILES = 160
LAT = 20480
COLS = 128


def draw_band_shift(key, part):
    base = jax.random.fold_in(key, 11)
    key_a, key_b, key_c = jax.random.split(base, 3)
    values = jax.random.randint(key_a, (SECTIONS, LAT_TILES), -1, 2)
    low_at = jax.random.randint(key_b, (SECTIONS,), 0, LAT_TILES)
    high_at = (low_at + 1 + jax.random.randint(key_c, (SECTIONS,), 0, LAT_TILES - 1)) % LAT_TILES
    column_ids = jnp.arange(LAT_TILES)[None, :]
    values = jnp.where(column_ids == low_at[:, None], -1, values)
    values = jnp.where(column_ids == high_at[:, None], 1, values)
    return values.astype(jnp.int32)


def shard_levels(stream_key, dims, cuts, least, high):
    level = 1.0
    for dim, parts in cuts:
        heights = jax.random.uniform(jax.random.fold_in(jax.random.fold_in(stream_key, 6), dim), (parts,), jnp.float32, least / len(cuts), high / len(cuts))
        level = level * jnp.repeat(jnp.exp(heights), dims[dim] // parts).reshape((-1,) + (1,) * (len(dims) - 1 - dim))
    return level


def noise(own_key, shape, scale, most, shards=(), kind=jnp.bfloat16):
    loudness = shard_levels(own_key, shape, shards, -0.22, 0.18) if shards else 1.0
    array = jax.random.normal(own_key, shape, jnp.float32) * scale * loudness
    return jnp.minimum(jnp.maximum(array, -most), most).astype(kind)


def setup_inputs(seed: int = 0) -> dict:
    key_of = jax.random.split(jax.random.key(seed), 8)
    operator = noise(key_of[0], (SECTIONS, LAT_TILES, 9, 2 * TILE, TILE), (2 * 9 * TILE) ** -0.5, 0.125, ((0, 8), (1, 32)), jnp.float32)
    band_shift = draw_band_shift(jax.random.fold_in(key_of[7], 71), 0)
    reflectivity = jnp.clip(jax.random.uniform(key_of[2], (SECTIONS, LAT), jnp.float32, -0.4, 0.4) * shard_levels(key_of[2], (SECTIONS, LAT), ((0, 8), (1, 32)), -0.4, 0.0), -0.4, 0.4)
    up_stored = noise(key_of[3], (SECTIONS, LAT, COLS), 1.0, 6.0, ((0, 8), (1, 32)), jnp.float32)
    down_stored = noise(key_of[4], (SECTIONS, LAT, COLS), 1.0, 6.0, ((0, 8), (1, 32)), jnp.float32)
    sources = noise(key_of[5], (LAT, COLS), 1.0, 6.0, ((0, 32),), jnp.float32)
    assignment = jax.random.permutation(key_of[6], 2 * SHOTS).astype(jnp.int32)
    return {"operator": operator, "band_shift": band_shift, "reflectivity": reflectivity, "up_stored": up_stored, "down_stored": down_stored, "sources": sources, "assignment": assignment}


def combine_parts(real_rows, imag_rows):
    col_count = real_rows.shape[-1]
    shape_in = real_rows.shape[:-1] + (col_count // (2 * SHOTS), 2, SHOTS)
    real_terms = real_rows.reshape(shape_in)
    imag_terms = imag_rows.reshape(shape_in)
    real_part = real_terms[..., 0, :] - imag_terms[..., 1, :]
    imag_part = real_terms[..., 1, :] + imag_terms[..., 0, :]
    return jnp.stack([real_part, imag_part], axis=-2).reshape(real_rows.shape)


def propagate(extrapolator, offsets, wavefield):
    tile_count = extrapolator.shape[0]
    col_count = wavefield.shape[1]
    padded = jnp.pad(wavefield, ((5 * TILE, 5 * TILE), (0, 0)))
    blocks = padded.reshape(tile_count + 10, TILE, col_count)
    starts = jnp.arange(tile_count, dtype=jnp.int32) + 1 + offsets.astype(jnp.int32)
    banded = jax.vmap(lambda begin_at: lax.dynamic_slice_in_dim(blocks, begin_at, 9, 0))(starts)
    product = jnp.einsum("gkab,gkbc->gac", extrapolator, banded, precision=lax.Precision.HIGHEST)
    real_rows = product[:, :TILE].reshape(tile_count * TILE, col_count)
    imag_rows = product[:, TILE:].reshape(tile_count * TILE, col_count)
    return combine_parts(real_rows, imag_rows)


def reference(operator, band_shift, reflectivity, up_stored, down_stored, sources, assignment):
    lateral = sources.shape[0]
    real_src = jnp.take(sources[:, :2 * SHOTS], assignment, axis=1)
    imag_src = jnp.take(sources[:, 2 * SHOTS:], assignment, axis=1)
    entering = jnp.stack([real_src.reshape(lateral, 2, SHOTS), imag_src.reshape(lateral, 2, SHOTS)], axis=2).reshape(lateral, 4 * SHOTS)
    down_list = []
    for section in range(SECTIONS):
        reflect_col = reflectivity[section][:, None]
        joined = (1.0 + reflect_col) * entering - reflect_col * up_stored[section]
        entering = propagate(operator[section], band_shift[section], joined)
        down_list.append(entering)
    rising = jnp.zeros_like(sources)
    up_list = [None] * SECTIONS
    for section in reversed(range(SECTIONS)):
        reflect_col = reflectivity[section][:, None]
        joined = (1.0 - reflect_col) * rising + reflect_col * down_stored[section]
        rising = propagate(operator[section], band_shift[section], joined)
        up_list[section] = rising
    return jnp.stack(down_list), jnp.stack(up_list)
```

```python
import jax
import jax.numpy as jnp
from jax import lax
from jax.experimental import pallas as pl
from jax.experimental.pallas import tpu as pltpu
from jax.sharding import PartitionSpec as P

TILE = 128
SHOTS = 32
GROUP = 8
ROWS = 2 * GROUP
CHUNKS = 2 * SHOTS // GROUP
PER_BATCH = SHOTS // GROUP
COLS = 4 * SHOTS
DOWN, UP = 0, 1
MESH = pl.DeviceIdType.MESH


def column_group(chunk, part):
    return (chunk // PER_BATCH) * 2 * PER_BATCH + part * PER_BATCH + chunk % PER_BATCH


def kernel(
    sections,
    lat_devices,
    operator,
    shift,
    reflect,
    up_stored,
    down_stored,
    sources,
    assignment,
    down_out,
    up_out,
    raw,
    high,
    low,
    up_rows,
    down_rows,
    source_rows,
    local,
    weight,
    arrived,
    result,
    split,
    load_sem,
    raw_sem,
    local_send,
    local_recv,
    weight_send,
    weight_recv,
    field_send,
    field_recv,
):
    depth = lax.axis_index("depth")
    lat = lax.axis_index("lat")
    tiles = raw.shape[0]
    width = tiles * TILE

    loads = [
        pltpu.make_async_copy(source, target, load_sem.at[n])
        for n, (source, target) in enumerate(
            [
                (sources, source_rows),
                (up_stored.at[0], up_rows),
                (down_stored.at[0], down_rows),
            ]
        )
    ]
    raw_loads = [
        pltpu.make_async_copy(operator.at[0, g], raw.at[g], raw_sem.at[g]) for g in range(tiles)
    ]
    for copy in loads:
        copy.start()
    for copy in raw_loads:
        copy.start()

    def lat_ok(step):
        return (lat + step >= 0) & (lat + step < lat_devices)

    def depth_ok(step):
        return (depth + step >= 0) & (depth + step < sections)

    barrier = pltpu.get_barrier_semaphore()
    greeted = 0
    for down_by in (-1, 0, 1):
        for right_by in (-1, 0, 1):
            if (down_by, right_by) == (0, 0):
                continue
            ok = lat_ok(right_by) & depth_ok(down_by)
            greeted = greeted + ok.astype(jnp.int32)

            @pl.when(ok)
            def _():
                pl.semaphore_signal(
                    barrier,
                    inc=1,
                    device_id=(depth + down_by, lat + right_by),
                    device_id_type=MESH,
                )

    strength = reflect[...]
    weight[1] = jnp.broadcast_to(strength, (8, width))

    def put_local(which, rows, scale, offset=None):
        for g in range(tiles):
            flipped = jnp.transpose(rows[g * TILE : (g + 1) * TILE, :])
            here = slice(g * TILE, (g + 1) * TILE)
            for chunk in range(CHUNKS):
                for part in range(2):
                    group = column_group(chunk, part)
                    value = flipped[group * GROUP : (group + 1) * GROUP] * scale[:, here]
                    if offset is not None:
                        value = value + local[which, chunk, 1, part * GROUP : (part + 1) * GROUP, here]
                    local[which, chunk, 1, part * GROUP : (part + 1) * GROUP, here] = value

    loads[0].wait()
    loads[1].wait()
    put_local(DOWN, up_rows[...], -strength)

    @pl.when(depth == 0)
    def _():
        lanes = lax.broadcasted_iota(jnp.int32, (1, COLS), 1)
        wanted = jnp.zeros((1, COLS), jnp.int32)
        for slot in range(2 * SHOTS):
            column = (slot // SHOTS) * 2 * SHOTS + slot % SHOTS
            wanted = jnp.where(lanes == column, assignment[slot], wanted)
            wanted = jnp.where(lanes == column + SHOTS, assignment[slot] + 2 * SHOTS, wanted)
        chosen = (lax.broadcasted_iota(jnp.int32, (COLS, COLS), 0) == wanted).astype(jnp.float32)
        entering = jnp.dot(
            source_rows[...],
            chosen,
            precision=lax.Precision.HIGHEST,
            preferred_element_type=jnp.float32,
        )
        put_local(DOWN, entering, 1.0 + strength, offset=True)
        arrived[DOWN] = jnp.zeros(arrived.shape[1:], jnp.float32)

    loads[2].wait()
    put_local(UP, down_rows[...], strength)

    @pl.when(depth == sections - 1)
    def _():
        arrived[UP] = jnp.zeros(arrived.shape[1:], jnp.float32)

    for edge, slot in ((0, 0), (lat_devices - 1, 2)):

        @pl.when(lat == edge)
        def _():
            weight[slot] = jnp.zeros(weight.shape[1:], jnp.float32)

            def clear(which, _):
                for chunk in range(CHUNKS):
                    local[which, chunk, slot] = jnp.zeros((ROWS, width), jnp.float32)
                    arrived[which, chunk, slot] = jnp.zeros((ROWS, width), jnp.float32)
                return 0

            lax.fori_loop(0, 2, clear, 0)

    pl.semaphore_wait(barrier, greeted)

    def weight_copy(step):
        slot = 1 - step
        return pltpu.make_async_remote_copy(
            src_ref=weight.at[1],
            dst_ref=weight.at[slot],
            send_sem=weight_send.at[slot],
            recv_sem=weight_recv.at[slot],
            device_id=(depth, lat + step),
            device_id_type=MESH,
        )

    def local_copy(which, chunk, step):
        slot = 1 - step
        return pltpu.make_async_remote_copy(
            src_ref=local.at[which, chunk, 1],
            dst_ref=local.at[which, chunk, slot],
            send_sem=local_send.at[which, chunk, slot],
            recv_sem=local_recv.at[which, chunk, slot],
            device_id=(depth, lat + step),
            device_id_type=MESH,
        )

    def field_copy(which, chunk, step):
        slot = 1 - step
        return pltpu.make_async_remote_copy(
            src_ref=result.at[which, chunk],
            dst_ref=arrived.at[which, chunk, slot],
            send_sem=field_send.at[which, chunk, slot],
            recv_sem=field_recv.at[which, chunk, slot],
            device_id=(depth + 1 - 2 * which, lat + step),
            device_id_type=MESH,
        )

    early = jnp.where(2 * depth < sections, DOWN, UP)
    lag = jnp.where((depth == sections // 2 - 1) | (depth == sections // 2), 3, CHUNKS)

    def event(number):
        mixed = (number >= lag) & (number < 2 * CHUNKS - lag)
        turn = (number - lag) // 2
        odd = (number - lag) % 2
        of_early = (number < lag) | (mixed & (odd == 1))
        chunk = jnp.where(
            number < lag,
            number,
            jnp.where(mixed, jnp.where(odd == 1, lag + turn, turn), number - CHUNKS),
        )
        return jnp.where(of_early, early, 1 - early), chunk

    for step in (-1, 1):

        @pl.when(lat_ok(step))
        def _():
            weight_copy(step).start()

    def send_local(number, _):
        which, chunk = jnp.where(number < CHUNKS, early, 1 - early), number % CHUNKS
        for step in (-1, 1):

            @pl.when(lat_ok(step))
            def _():
                local_copy(which, chunk, step).start()

        return 0

    lax.fori_loop(0, 2 * CHUNKS, send_local, 0)

    for copy in raw_loads:
        copy.wait()

    def prepare(g, _):
        for k in range(9):
            flipped = jnp.transpose(raw[g, k])
            lead = flipped.astype(jnp.bfloat16)
            here = slice(k * TILE, (k + 1) * TILE)
            high[g, here, :] = lead
            low[g, here, :] = (flipped - lead.astype(jnp.float32)).astype(jnp.bfloat16)
        return 0

    lax.fori_loop(0, tiles, prepare, 0)

    for step in (-1, 1):

        @pl.when(lat_ok(step))
        def _():
            weight_copy(step).wait_send()

    for step in (-1, 1):

        @pl.when(lat_ok(-step))
        def _():
            weight_copy(step).wait_recv()

    def run(number, _):
        which, chunk = event(number)
        has_in = depth_ok(2 * which - 1)
        has_out = depth_ok(1 - 2 * which)
        sign = (1 - 2 * which).astype(jnp.float32)
        for step in (-1, 1):

            @pl.when(lat_ok(-step))
            def _():
                local_copy(which, chunk, step).wait_recv()

        for step in (0, -1, 1):

            @pl.when(has_in & lat_ok(-step))
            def _():
                field_copy(which, chunk, step).wait_recv()

        for slot in range(3):
            scale = 1.0 + sign * weight[slot]
            scale = jnp.concatenate([scale, scale], axis=0)
            field = local[which, chunk, slot] + scale * arrived[which, chunk, slot]
            lead = field.astype(jnp.bfloat16)
            here = slice(slot * width, (slot + 1) * width)
            split[:ROWS, here] = lead
            split[ROWS:, here] = (field - lead.astype(jnp.float32)).astype(jnp.bfloat16)
        for g in range(tiles):
            start = (g + 1 + shift[0, g]) * TILE
            window = split[:, pl.ds(start, 9 * TILE)]
            both = jnp.dot(window, high[g], preferred_element_type=jnp.float32)
            rest = jnp.dot(window[:ROWS], low[g], preferred_element_type=jnp.float32)
            total = both[:ROWS] + both[ROWS:] + rest
            here = slice(g * TILE, (g + 1) * TILE)
            result[which, chunk, :GROUP, here] = total[:GROUP, :TILE] - total[GROUP:, TILE:]
            result[which, chunk, GROUP:, here] = total[GROUP:, :TILE] + total[:GROUP, TILE:]
        for step in (0, -1, 1):

            @pl.when(has_out & lat_ok(step))
            def _():
                field_copy(which, chunk, step).start()

        return 0

    lax.fori_loop(0, 2 * CHUNKS, run, 0)

    for which, out in ((DOWN, down_out), (UP, up_out)):
        for g in range(tiles):
            here = slice(g * TILE, (g + 1) * TILE)
            groups = [None] * (2 * CHUNKS)
            for chunk in range(CHUNKS):
                for part in range(2):
                    groups[column_group(chunk, part)] = result[
                        which, chunk, part * GROUP : (part + 1) * GROUP, here
                    ]
            out[here, :] = jnp.transpose(jnp.concatenate(groups, axis=0))

    def finish(number, _):
        which, chunk = number // CHUNKS, number % CHUNKS
        for step in (-1, 1):

            @pl.when(lat_ok(step))
            def _():
                local_copy(which, chunk, step).wait_send()

        for step in (0, -1, 1):

            @pl.when(depth_ok(1 - 2 * which) & lat_ok(step))
            def _():
                field_copy(which, chunk, step).wait_send()

        return 0

    lax.fori_loop(0, 2 * CHUNKS, finish, 0)


def solution(mesh):
    sections = mesh.shape["depth"]
    lat_devices = mesh.shape["lat"]

    def shards(operator, band_shift, reflectivity, up_stored, down_stored, sources, assignment):
        tiles = operator.shape[1]
        width = tiles * TILE
        anywhere = pl.BlockSpec(memory_space=pl.ANY)
        in_vmem = pl.BlockSpec(memory_space=pltpu.VMEM)
        in_smem = pl.BlockSpec(memory_space=pltpu.SMEM)
        dma = pltpu.SemaphoreType.DMA

        def body(*refs):
            kernel(sections, lat_devices, *refs)

        down, up = pl.pallas_call(
            body,
            out_shape=[jax.ShapeDtypeStruct((width, COLS), jnp.float32)] * 2,
            in_specs=[anywhere, in_smem, in_vmem, anywhere, anywhere, anywhere, in_smem],
            out_specs=[in_vmem, in_vmem],
            scratch_shapes=[
                pltpu.VMEM((tiles, 9, 2 * TILE, TILE), jnp.float32),
                pltpu.VMEM((tiles, 9 * TILE, 2 * TILE), jnp.bfloat16),
                pltpu.VMEM((tiles, 9 * TILE, 2 * TILE), jnp.bfloat16),
                pltpu.VMEM((width, COLS), jnp.float32),
                pltpu.VMEM((width, COLS), jnp.float32),
                pltpu.VMEM((width, COLS), jnp.float32),
                pltpu.VMEM((2, CHUNKS, 3, ROWS, width), jnp.float32),
                pltpu.VMEM((3, 8, width), jnp.float32),
                pltpu.VMEM((2, CHUNKS, 3, ROWS, width), jnp.float32),
                pltpu.VMEM((2, CHUNKS, ROWS, width), jnp.float32),
                pltpu.VMEM((2 * ROWS, 3 * width), jnp.bfloat16),
                dma((3,)),
                dma((tiles,)),
                dma((2, CHUNKS, 3)),
                dma((2, CHUNKS, 3)),
                dma((3,)),
                dma((3,)),
                dma((2, CHUNKS, 3)),
                dma((2, CHUNKS, 3)),
            ],
            compiler_params=pltpu.CompilerParams(
                collective_id=0, has_side_effects=True, vmem_limit_bytes=60 * 2**20
            ),
            name="round_trip",
        )(operator, band_shift, reflectivity, up_stored, down_stored, sources, assignment)
        return down[None], up[None]

    return jax.shard_map(
        shards,
        mesh=mesh,
        in_specs=(
            P("depth", "lat", None, None, None),
            P("depth", "lat"),
            P("depth", "lat"),
            P("depth", "lat", None),
            P("depth", "lat", None),
            P("lat", None),
            P(),
        ),
        out_specs=(P("depth", "lat", None), P("depth", "lat", None)),
        check_vma=False,
    )
```

```python
import jax
import jax.numpy as jnp
from jax import lax
from jax.experimental import pallas as pl
from jax.experimental.pallas import tpu as pltpu
from jax.sharding import PartitionSpec as P

TILE = 128
SHOTS = 32
GROUP = 8
ROWS = 2 * GROUP
CHUNKS = 2 * SHOTS // GROUP
PER_BATCH = SHOTS // GROUP
COLS = 4 * SHOTS
DOWN, UP = 0, 1
MESH = pl.DeviceIdType.MESH


def column_group(chunk, part):
    return (chunk // PER_BATCH) * 2 * PER_BATCH + part * PER_BATCH + chunk % PER_BATCH


def kernel(
    sections,
    lat_devices,
    operator,
    shift,
    reflect,
    up_stored,
    down_stored,
    sources,
    assignment,
    result,
    raw,
    high,
    low,
    up_rows,
    down_rows,
    source_rows,
    mine,
    local,
    weight,
    terms,
    arrived,
    leaving,
    split,
    load_sem,
    raw_sem,
    term_send,
    term_recv,
    weight_send,
    weight_recv,
    field_send,
    field_recv,
):
    depth = lax.axis_index("depth")
    lat = lax.axis_index("lat")
    tiles = raw.shape[0]
    width = tiles * TILE

    loads = [
        pltpu.make_async_copy(source, target, load_sem.at[n])
        for n, (source, target) in enumerate(
            [
                (sources, source_rows),
                (up_stored.at[0], up_rows),
                (down_stored.at[0], down_rows),
            ]
        )
    ]
    raw_loads = [
        pltpu.make_async_copy(operator.at[0, g], raw.at[g], raw_sem.at[g]) for g in range(tiles)
    ]
    for copy in loads:
        copy.start()
    for copy in raw_loads:
        copy.start()

    def lat_ok(step):
        return (lat + step >= 0) & (lat + step < lat_devices)

    def depth_ok(step):
        return (depth + step >= 0) & (depth + step < sections)

    barrier = pltpu.get_barrier_semaphore()
    greeted = 0
    for down_by in (-1, 0, 1):
        for right_by in (-1, 0, 1):
            if (down_by, right_by) == (0, 0):
                continue
            ok = lat_ok(right_by) & depth_ok(down_by)
            greeted = greeted + ok.astype(jnp.int32)

            @pl.when(ok)
            def _():
                pl.semaphore_signal(
                    barrier,
                    inc=1,
                    device_id=(depth + down_by, lat + right_by),
                    device_id_type=MESH,
                )

    strength = reflect[...]
    mine[...] = jnp.broadcast_to(strength, mine.shape)

    def pieces(rows):
        for g in range(tiles):
            flipped = jnp.transpose(rows[g * TILE : (g + 1) * TILE, :])
            here = slice(g * TILE, (g + 1) * TILE)
            for chunk in range(CHUNKS):
                for part in range(2):
                    group = column_group(chunk, part)
                    place = slice(part * GROUP, (part + 1) * GROUP)
                    yield chunk, place, here, flipped[group * GROUP : (group + 1) * GROUP]

    loads[0].wait()
    loads[1].wait()
    for chunk, place, here, value in pieces(up_rows[...]):
        local[DOWN, chunk, place, here] = -strength[:, here] * value

    @pl.when(depth == 0)
    def _():
        lanes = lax.broadcasted_iota(jnp.int32, (1, COLS), 1)
        wanted = jnp.zeros((1, COLS), jnp.int32)
        for slot in range(2 * SHOTS):
            column = (slot // SHOTS) * 2 * SHOTS + slot % SHOTS
            wanted = jnp.where(lanes == column, assignment[slot], wanted)
            wanted = jnp.where(lanes == column + SHOTS, assignment[slot] + 2 * SHOTS, wanted)
        chosen = (lax.broadcasted_iota(jnp.int32, (COLS, COLS), 0) == wanted).astype(jnp.float32)
        entering = jnp.dot(
            source_rows[...],
            chosen,
            precision=lax.Precision.HIGHEST,
            preferred_element_type=jnp.float32,
        )
        for chunk, place, here, value in pieces(entering):
            arrived[DOWN, chunk, 1, place, here] = (
                local[DOWN, chunk, place, here] + (1.0 + strength[:, here]) * value
            )

    loads[2].wait()
    for chunk, place, here, value in pieces(down_rows[...]):
        local[UP, chunk, place, here] = strength[:, here] * value

    @pl.when(depth == sections - 1)
    def _():
        for chunk in range(CHUNKS):
            arrived[UP, chunk, 1] = local[UP, chunk]

    for edge, slot in ((0, 0), (lat_devices - 1, 2)):

        @pl.when(lat == edge)
        def _():
            def clear(which, _):
                for chunk in range(CHUNKS):
                    arrived[which, chunk, slot] = jnp.zeros((ROWS, width), jnp.float32)
                return 0

            lax.fori_loop(0, 2, clear, 0)

    pl.semaphore_wait(barrier, greeted)

    def term_copy(which, half):
        some = pl.ds(half * (CHUNKS // 2), CHUNKS // 2)
        return pltpu.make_async_remote_copy(
            src_ref=local.at[which, some],
            dst_ref=terms.at[which, some],
            send_sem=term_send.at[which, half],
            recv_sem=term_recv.at[which, half],
            device_id=(depth - 1 + 2 * which, lat),
            device_id_type=MESH,
        )

    def weight_copy(which):
        return pltpu.make_async_remote_copy(
            src_ref=mine,
            dst_ref=weight.at[which],
            send_sem=weight_send.at[which],
            recv_sem=weight_recv.at[which],
            device_id=(depth - 1 + 2 * which, lat),
            device_id_type=MESH,
        )

    def first_copy(which, chunk, step):
        slot = 1 - step
        return pltpu.make_async_remote_copy(
            src_ref=arrived.at[which, chunk, 1],
            dst_ref=arrived.at[which, chunk, slot],
            send_sem=field_send.at[1 - which, chunk, slot],
            recv_sem=field_recv.at[which, chunk, slot],
            device_id=(depth, lat + step),
            device_id_type=MESH,
        )

    def field_copy(which, chunk, step):
        slot = 1 - step
        return pltpu.make_async_remote_copy(
            src_ref=leaving.at[which, chunk],
            dst_ref=arrived.at[which, chunk, slot],
            send_sem=field_send.at[which, chunk, slot],
            recv_sem=field_recv.at[which, chunk, slot],
            device_id=(depth + 1 - 2 * which, lat + step),
            device_id_type=MESH,
        )

    early = jnp.where(2 * depth < sections, DOWN, UP)
    lag = jnp.where((depth == sections // 2 - 1) | (depth == sections // 2), 3, CHUNKS)

    def event(number):
        mixed = (number >= lag) & (number < 2 * CHUNKS - lag)
        turn = (number - lag) // 2
        odd = (number - lag) % 2
        of_early = (number < lag) | (mixed & (odd == 1))
        chunk = jnp.where(
            number < lag,
            number,
            jnp.where(mixed, jnp.where(odd == 1, lag + turn, turn), number - CHUNKS),
        )
        return jnp.where(of_early, early, 1 - early), chunk

    at_end = (depth == 0) | (depth == sections - 1)

    @pl.when(at_end)
    def _():
        def send_first(chunk, _):
            for step in (-1, 1):

                @pl.when(lat_ok(step))
                def _():
                    first_copy(early, chunk, step).start()

            return 0

        lax.fori_loop(0, CHUNKS, send_first, 0)

    for which in (DOWN, UP):

        @pl.when(depth_ok(2 * which - 1))
        def _():
            weight_copy(which).start()

    for half in range(2):
        for which in (DOWN, UP):

            @pl.when(depth_ok(2 * which - 1))
            def _():
                term_copy(which, half).start()

    for copy in raw_loads:
        copy.wait()

    def prepare(g, _):
        for k in range(9):
            flipped = jnp.transpose(raw[g, k])
            lead = flipped.astype(jnp.bfloat16)
            here = slice(k * TILE, (k + 1) * TILE)
            high[g, here, :] = lead
            low[g, here, :] = (flipped - lead.astype(jnp.float32)).astype(jnp.bfloat16)
        return 0

    lax.fori_loop(0, tiles, prepare, 0)

    for which in (DOWN, UP):

        @pl.when(depth_ok(1 - 2 * which))
        def _():
            weight_copy(which).wait_recv()

    def run(number, _):
        which, chunk = event(number)
        has_in = depth_ok(2 * which - 1)
        has_out = depth_ok(1 - 2 * which)
        sign = (1 - 2 * which).astype(jnp.float32)

        @pl.when(has_in)
        def _():
            field_copy(which, chunk, 0).wait_recv()

        for step in (-1, 1):

            @pl.when(lat_ok(-step))
            def _():
                field_copy(which, chunk, step).wait_recv()

        for slot in range(3):
            field = arrived[which, chunk, slot]
            lead = field.astype(jnp.bfloat16)
            here = slice(slot * width, (slot + 1) * width)
            split[:ROWS, here] = lead
            split[ROWS:, here] = (field - lead.astype(jnp.float32)).astype(jnp.bfloat16)

        @pl.when(has_out & (chunk % (CHUNKS // 2) == 0))
        def _():
            term_copy(which, chunk // (CHUNKS // 2)).wait_recv()

        for g in range(tiles):
            start = (g + 1 + shift[0, g]) * TILE
            window = split[:, pl.ds(start, 9 * TILE)]
            both = jnp.dot(window, high[g], preferred_element_type=jnp.float32)
            rest = jnp.dot(window[:ROWS], low[g], preferred_element_type=jnp.float32)
            total = both[:ROWS] + both[ROWS:] + rest
            here = slice(g * TILE, (g + 1) * TILE)
            result[which, chunk, :GROUP, here] = total[:GROUP, :TILE] - total[GROUP:, TILE:]
            result[which, chunk, GROUP:, here] = total[GROUP:, :TILE] + total[:GROUP, TILE:]

        @pl.when(has_out)
        def _():
            scale = 1.0 + sign * weight[which]
            scale = jnp.concatenate([scale, scale], axis=0)
            leaving[which, chunk] = terms[which, chunk] + scale * result[which, chunk]

        for step in (0, -1, 1):

            @pl.when(has_out & lat_ok(step))
            def _():
                field_copy(which, chunk, step).start()

        return 0

    lax.fori_loop(0, 2 * CHUNKS, run, 0)

    for which in (DOWN, UP):

        @pl.when(depth_ok(2 * which - 1))
        def _():
            weight_copy(which).wait_send()
            for half in range(2):
                term_copy(which, half).wait_send()

    @pl.when(at_end)
    def _():
        def finish_first(chunk, _):
            for step in (-1, 1):

                @pl.when(lat_ok(step))
                def _():
                    first_copy(early, chunk, step).wait_send()

            return 0

        lax.fori_loop(0, CHUNKS, finish_first, 0)

    def finish(number, _):
        which, chunk = number // CHUNKS, number % CHUNKS
        for step in (0, -1, 1):

            @pl.when(depth_ok(1 - 2 * which) & lat_ok(step))
            def _():
                field_copy(which, chunk, step).wait_send()

        return 0

    lax.fori_loop(0, 2 * CHUNKS, finish, 0)


def unpack(result, down_out, up_out):
    for which, out in ((DOWN, down_out), (UP, up_out)):
        for g in range(out.shape[0] // TILE):
            here = slice(g * TILE, (g + 1) * TILE)
            groups = [None] * (2 * CHUNKS)
            for chunk in range(CHUNKS):
                for part in range(2):
                    groups[column_group(chunk, part)] = result[
                        which, chunk, part * GROUP : (part + 1) * GROUP, here
                    ]
            out[here, :] = jnp.transpose(jnp.concatenate(groups, axis=0))


def solution(mesh):
    sections = mesh.shape["depth"]
    lat_devices = mesh.shape["lat"]

    def shards(operator, band_shift, reflectivity, up_stored, down_stored, sources, assignment):
        tiles = operator.shape[1]
        width = tiles * TILE
        anywhere = pl.BlockSpec(memory_space=pl.ANY)
        in_vmem = pl.BlockSpec(memory_space=pltpu.VMEM)
        in_smem = pl.BlockSpec(memory_space=pltpu.SMEM)
        dma = pltpu.SemaphoreType.DMA

        def body(*refs):
            kernel(sections, lat_devices, *refs)

        result = pl.pallas_call(
            body,
            out_shape=jax.ShapeDtypeStruct((2, CHUNKS, ROWS, width), jnp.float32),
            in_specs=[anywhere, in_smem, in_vmem, anywhere, anywhere, anywhere, in_smem],
            out_specs=in_vmem,
            scratch_shapes=[
                pltpu.VMEM((tiles, 9, 2 * TILE, TILE), jnp.float32),
                pltpu.VMEM((tiles, 9 * TILE, 2 * TILE), jnp.bfloat16),
                pltpu.VMEM((tiles, 9 * TILE, 2 * TILE), jnp.bfloat16),
                pltpu.VMEM((width, COLS), jnp.float32),
                pltpu.VMEM((width, COLS), jnp.float32),
                pltpu.VMEM((width, COLS), jnp.float32),
                pltpu.VMEM((8, width), jnp.float32),
                pltpu.VMEM((2, CHUNKS, ROWS, width), jnp.float32),
                pltpu.VMEM((2, 8, width), jnp.float32),
                pltpu.VMEM((2, CHUNKS, ROWS, width), jnp.float32),
                pltpu.VMEM((2, CHUNKS, 3, ROWS, width), jnp.float32),
                pltpu.VMEM((2, CHUNKS, ROWS, width), jnp.float32),
                pltpu.VMEM((2 * ROWS, 3 * width), jnp.bfloat16),
                dma((3,)),
                dma((tiles,)),
                dma((2, 2)),
                dma((2, 2)),
                dma((2,)),
                dma((2,)),
                dma((2, CHUNKS, 3)),
                dma((2, CHUNKS, 3)),
            ],
            compiler_params=pltpu.CompilerParams(
                collective_id=0, has_side_effects=True, vmem_limit_bytes=60 * 2**20
            ),
            name="round_trip",
        )(operator, band_shift, reflectivity, up_stored, down_stored, sources, assignment)
        down, up = pl.pallas_call(
            unpack,
            out_shape=[jax.ShapeDtypeStruct((width, COLS), jnp.float32)] * 2,
            in_specs=[in_vmem],
            out_specs=[in_vmem, in_vmem],
            name="unpack",
        )(result)
        return down[None], up[None]

    return jax.shard_map(
        shards,
        mesh=mesh,
        in_specs=(
            P("depth", "lat", None, None, None),
            P("depth", "lat"),
            P("depth", "lat"),
            P("depth", "lat", None),
            P("depth", "lat", None),
            P("lat", None),
            P(),
        ),
        out_specs=(P("depth", "lat", None), P("depth", "lat", None)),
        check_vma=False,
    )
```

```python
import jax
import jax.numpy as jnp
from jax import lax
from jax.experimental import pallas as pl
from jax.experimental.pallas import tpu as pltpu
from jax.sharding import PartitionSpec as P

TILE = 128
SHOTS = 32
GROUP = 8
ROWS = 2 * GROUP
CHUNKS = 2 * SHOTS // GROUP
PER_BATCH = SHOTS // GROUP
COLS = 4 * SHOTS
DOWN, UP = 0, 1
WINDOW = 2
MESH = pl.DeviceIdType.MESH


def column_group(chunk, part):
    return (chunk // PER_BATCH) * 2 * PER_BATCH + part * PER_BATCH + chunk % PER_BATCH


def kernel(
    sections,
    lat_devices,
    operator,
    shift,
    reflect,
    up_stored,
    down_stored,
    sources,
    assignment,
    result,
    raw,
    high,
    low,
    up_rows,
    down_rows,
    source_rows,
    mine,
    local,
    weight,
    terms,
    arrived,
    leaving,
    split,
    load_sem,
    raw_sem,
    term_send,
    term_recv,
    weight_send,
    weight_recv,
    field_send,
    field_recv,
):
    depth = lax.axis_index("depth")
    lat = lax.axis_index("lat")
    tiles = raw.shape[0]
    width = tiles * TILE

    loads = [
        pltpu.make_async_copy(source, target, load_sem.at[n])
        for n, (source, target) in enumerate(
            [
                (sources, source_rows),
                (up_stored.at[0], up_rows),
                (down_stored.at[0], down_rows),
            ]
        )
    ]
    raw_loads = [
        pltpu.make_async_copy(operator.at[0, g], raw.at[g], raw_sem.at[g]) for g in range(tiles)
    ]
    for copy in loads:
        copy.start()
    for copy in raw_loads:
        copy.start()

    def lat_ok(step):
        return (lat + step >= 0) & (lat + step < lat_devices)

    def depth_ok(step):
        return (depth + step >= 0) & (depth + step < sections)

    barrier = pltpu.get_barrier_semaphore()
    greeted = 0
    for down_by in (-1, 0, 1):
        for right_by in (-1, 0, 1):
            if (down_by, right_by) == (0, 0):
                continue
            ok = lat_ok(right_by) & depth_ok(down_by)
            greeted = greeted + ok.astype(jnp.int32)

            @pl.when(ok)
            def _():
                pl.semaphore_signal(
                    barrier,
                    inc=1,
                    device_id=(depth + down_by, lat + right_by),
                    device_id_type=MESH,
                )

    strength = reflect[...]
    mine[...] = jnp.broadcast_to(strength, mine.shape)

    def pieces(rows):
        for g in range(tiles):
            flipped = jnp.transpose(rows[g * TILE : (g + 1) * TILE, :])
            here = slice(g * TILE, (g + 1) * TILE)
            for chunk in range(CHUNKS):
                for part in range(2):
                    group = column_group(chunk, part)
                    place = slice(part * GROUP, (part + 1) * GROUP)
                    yield chunk, place, here, flipped[group * GROUP : (group + 1) * GROUP]

    loads[0].wait()
    loads[1].wait()
    for chunk, place, here, value in pieces(up_rows[...]):
        local[DOWN, chunk, place, here] = -strength[:, here] * value

    @pl.when(depth == 0)
    def _():
        lanes = lax.broadcasted_iota(jnp.int32, (1, COLS), 1)
        wanted = jnp.zeros((1, COLS), jnp.int32)
        for slot in range(2 * SHOTS):
            column = (slot // SHOTS) * 2 * SHOTS + slot % SHOTS
            wanted = jnp.where(lanes == column, assignment[slot], wanted)
            wanted = jnp.where(lanes == column + SHOTS, assignment[slot] + 2 * SHOTS, wanted)
        chosen = (lax.broadcasted_iota(jnp.int32, (COLS, COLS), 0) == wanted).astype(jnp.float32)
        entering = jnp.dot(
            source_rows[...],
            chosen,
            precision=lax.Precision.HIGHEST,
            preferred_element_type=jnp.float32,
        )
        for chunk, place, here, value in pieces(entering):
            arrived[DOWN, chunk, 1, place, here] = (
                local[DOWN, chunk, place, here] + (1.0 + strength[:, here]) * value
            )

    loads[2].wait()
    for chunk, place, here, value in pieces(down_rows[...]):
        local[UP, chunk, place, here] = strength[:, here] * value

    @pl.when(depth == sections - 1)
    def _():
        for chunk in range(CHUNKS):
            arrived[UP, chunk, 1] = local[UP, chunk]

    for edge, slot in ((0, 0), (lat_devices - 1, 2)):

        @pl.when(lat == edge)
        def _():
            def clear(which, _):
                for chunk in range(CHUNKS):
                    arrived[which, chunk, slot] = jnp.zeros((ROWS, width), jnp.float32)
                return 0

            lax.fori_loop(0, 2, clear, 0)

    pl.semaphore_wait(barrier, greeted)

    def term_copy(which, half):
        some = pl.ds(half * (CHUNKS // 2), CHUNKS // 2)
        return pltpu.make_async_remote_copy(
            src_ref=local.at[which, some],
            dst_ref=terms.at[which, some],
            send_sem=term_send.at[which, half],
            recv_sem=term_recv.at[which, half],
            device_id=(depth - 1 + 2 * which, lat),
            device_id_type=MESH,
        )

    def weight_copy(which):
        return pltpu.make_async_remote_copy(
            src_ref=mine,
            dst_ref=weight.at[which],
            send_sem=weight_send.at[which],
            recv_sem=weight_recv.at[which],
            device_id=(depth - 1 + 2 * which, lat),
            device_id_type=MESH,
        )

    def first_copy(which, chunk, step):
        slot = 1 - step
        return pltpu.make_async_remote_copy(
            src_ref=arrived.at[which, chunk, 1],
            dst_ref=arrived.at[which, chunk, slot],
            send_sem=field_send.at[1 - which, chunk, slot],
            recv_sem=field_recv.at[which, chunk, slot],
            device_id=(depth, lat + step),
            device_id_type=MESH,
        )

    def field_copy(which, chunk, step):
        slot = 1 - step
        return pltpu.make_async_remote_copy(
            src_ref=leaving.at[which, chunk],
            dst_ref=arrived.at[which, chunk, slot],
            send_sem=field_send.at[which, chunk, slot],
            recv_sem=field_recv.at[which, chunk, slot],
            device_id=(depth + 1 - 2 * which, lat + step),
            device_id_type=MESH,
        )

    early = jnp.where(2 * depth < sections, DOWN, UP)
    lag = jnp.where((depth == sections // 2 - 1) | (depth == sections // 2), 3, CHUNKS)

    def event(number):
        mixed = (number >= lag) & (number < 2 * CHUNKS - lag)
        turn = (number - lag) // 2
        odd = (number - lag) % 2
        of_early = (number < lag) | (mixed & (odd == 1))
        chunk = jnp.where(
            number < lag,
            number,
            jnp.where(mixed, jnp.where(odd == 1, lag + turn, turn), number - CHUNKS),
        )
        return jnp.where(of_early, early, 1 - early), chunk

    at_end = (depth == 0) | (depth == sections - 1)

    @pl.when(at_end)
    def _():
        def send_first(chunk, _):
            for step in (-1, 1):

                @pl.when(lat_ok(step))
                def _():
                    first_copy(early, chunk, step).start()

            return 0

        lax.fori_loop(0, 1, send_first, 0)

    for which in (DOWN, UP):

        @pl.when(depth_ok(2 * which - 1))
        def _():
            weight_copy(which).start()

    for half in range(2):
        for which in (DOWN, UP):

            @pl.when(depth_ok(2 * which - 1))
            def _():
                term_copy(which, half).start()

    for copy in raw_loads:
        copy.wait()

    def prepare(g, _):
        for k in range(9):
            flipped = jnp.transpose(raw[g, k])
            lead = flipped.astype(jnp.bfloat16)
            here = slice(k * TILE, (k + 1) * TILE)
            high[g, here, :] = lead
            low[g, here, :] = (flipped - lead.astype(jnp.float32)).astype(jnp.bfloat16)
        return 0

    lax.fori_loop(0, tiles, prepare, 0)

    for which in (DOWN, UP):

        @pl.when(depth_ok(1 - 2 * which))
        def _():
            weight_copy(which).wait_recv()

    def run(number, _):
        which, chunk = event(number)

        @pl.when(at_end & (which == early) & (chunk + 1 < CHUNKS))
        def _():
            for step in (-1, 1):

                @pl.when(lat_ok(step))
                def _():
                    first_copy(early, chunk + 1, step).start()

        has_in = depth_ok(2 * which - 1)
        has_out = depth_ok(1 - 2 * which)
        sign = (1 - 2 * which).astype(jnp.float32)

        @pl.when(has_in)
        def _():
            field_copy(which, chunk, 0).wait_recv()

        for step in (-1, 1):

            @pl.when(lat_ok(-step))
            def _():
                field_copy(which, chunk, step).wait_recv()

        for slot in range(3):
            field = arrived[which, chunk, slot]
            lead = field.astype(jnp.bfloat16)
            here = slice(slot * width, (slot + 1) * width)
            split[:ROWS, here] = lead
            split[ROWS:, here] = (field - lead.astype(jnp.float32)).astype(jnp.bfloat16)

        @pl.when(has_out & (chunk % (CHUNKS // 2) == 0))
        def _():
            term_copy(which, chunk // (CHUNKS // 2)).wait_recv()

        for g in range(tiles):
            start = (g + 1 + shift[0, g]) * TILE
            window = split[:, pl.ds(start, 9 * TILE)]
            both = jnp.dot(window, high[g], preferred_element_type=jnp.float32)
            rest = jnp.dot(window[:ROWS], low[g], preferred_element_type=jnp.float32)
            total = both[:ROWS] + both[ROWS:] + rest
            here = slice(g * TILE, (g + 1) * TILE)
            result[which, chunk, :GROUP, here] = total[:GROUP, :TILE] - total[GROUP:, TILE:]
            result[which, chunk, GROUP:, here] = total[GROUP:, :TILE] + total[:GROUP, TILE:]

        @pl.when(has_out)
        def _():
            scale = 1.0 + sign * weight[which]
            scale = jnp.concatenate([scale, scale], axis=0)
            leaving[which, chunk] = terms[which, chunk] + scale * result[which, chunk]

        for step in (0, -1, 1):

            @pl.when(has_out & lat_ok(step) & (chunk >= WINDOW))
            def _():
                field_copy(which, chunk - WINDOW, step).wait_send()

        for step in (0, -1, 1):

            @pl.when(has_out & lat_ok(step))
            def _():
                field_copy(which, chunk, step).start()

        return 0

    lax.fori_loop(0, 2 * CHUNKS, run, 0)

    for which in (DOWN, UP):

        @pl.when(depth_ok(2 * which - 1))
        def _():
            weight_copy(which).wait_send()
            for half in range(2):
                term_copy(which, half).wait_send()

    @pl.when(at_end)
    def _():
        def finish_first(chunk, _):
            for step in (-1, 1):

                @pl.when(lat_ok(step))
                def _():
                    first_copy(early, chunk, step).wait_send()

            return 0

        lax.fori_loop(0, CHUNKS, finish_first, 0)

    def finish(number, _):
        which, chunk = number // CHUNKS, number % CHUNKS
        for step in (0, -1, 1):

            @pl.when(depth_ok(1 - 2 * which) & lat_ok(step) & (chunk >= CHUNKS - WINDOW))
            def _():
                field_copy(which, chunk, step).wait_send()

        return 0

    lax.fori_loop(0, 2 * CHUNKS, finish, 0)


def unpack(result, down_out, up_out):
    for which, out in ((DOWN, down_out), (UP, up_out)):
        for g in range(out.shape[0] // TILE):
            here = slice(g * TILE, (g + 1) * TILE)
            groups = [None] * (2 * CHUNKS)
            for chunk in range(CHUNKS):
                for part in range(2):
                    groups[column_group(chunk, part)] = result[
                        which, chunk, part * GROUP : (part + 1) * GROUP, here
                    ]
            out[here, :] = jnp.transpose(jnp.concatenate(groups, axis=0))


def solution(mesh):
    sections = mesh.shape["depth"]
    lat_devices = mesh.shape["lat"]

    def shards(operator, band_shift, reflectivity, up_stored, down_stored, sources, assignment):
        tiles = operator.shape[1]
        width = tiles * TILE
        anywhere = pl.BlockSpec(memory_space=pl.ANY)
        in_vmem = pl.BlockSpec(memory_space=pltpu.VMEM)
        in_smem = pl.BlockSpec(memory_space=pltpu.SMEM)
        dma = pltpu.SemaphoreType.DMA

        def body(*refs):
            kernel(sections, lat_devices, *refs)

        result = pl.pallas_call(
            body,
            out_shape=jax.ShapeDtypeStruct((2, CHUNKS, ROWS, width), jnp.float32),
            in_specs=[anywhere, in_smem, in_vmem, anywhere, anywhere, anywhere, in_smem],
            out_specs=in_vmem,
            scratch_shapes=[
                pltpu.VMEM((tiles, 9, 2 * TILE, TILE), jnp.float32),
                pltpu.VMEM((tiles, 9 * TILE, 2 * TILE), jnp.bfloat16),
                pltpu.VMEM((tiles, 9 * TILE, 2 * TILE), jnp.bfloat16),
                pltpu.VMEM((width, COLS), jnp.float32),
                pltpu.VMEM((width, COLS), jnp.float32),
                pltpu.VMEM((width, COLS), jnp.float32),
                pltpu.VMEM((8, width), jnp.float32),
                pltpu.VMEM((2, CHUNKS, ROWS, width), jnp.float32),
                pltpu.VMEM((2, 8, width), jnp.float32),
                pltpu.VMEM((2, CHUNKS, ROWS, width), jnp.float32),
                pltpu.VMEM((2, CHUNKS, 3, ROWS, width), jnp.float32),
                pltpu.VMEM((2, CHUNKS, ROWS, width), jnp.float32),
                pltpu.VMEM((2 * ROWS, 3 * width), jnp.bfloat16),
                dma((3,)),
                dma((tiles,)),
                dma((2, 2)),
                dma((2, 2)),
                dma((2,)),
                dma((2,)),
                dma((2, CHUNKS, 3)),
                dma((2, CHUNKS, 3)),
            ],
            compiler_params=pltpu.CompilerParams(
                collective_id=0, has_side_effects=True, vmem_limit_bytes=60 * 2**20
            ),
            name="round_trip",
        )(operator, band_shift, reflectivity, up_stored, down_stored, sources, assignment)
        down, up = pl.pallas_call(
            unpack,
            out_shape=[jax.ShapeDtypeStruct((width, COLS), jnp.float32)] * 2,
            in_specs=[in_vmem],
            out_specs=[in_vmem, in_vmem],
            name="unpack",
        )(result)
        return down[None], up[None]

    return jax.shard_map(
        shards,
        mesh=mesh,
        in_specs=(
            P("depth", "lat", None, None, None),
            P("depth", "lat"),
            P("depth", "lat"),
            P("depth", "lat", None),
            P("depth", "lat", None),
            P("lat", None),
            P(),
        ),
        out_specs=(P("depth", "lat", None), P("depth", "lat", None)),
        check_vma=False,
    )
```

```python
import jax
import jax.numpy as jnp
from jax import lax
from jax.experimental import pallas as pl
from jax.experimental.pallas import tpu as pltpu
from jax.sharding import PartitionSpec as P

TILE = 128
SHOTS = 32
GROUP = 8
ROWS = 2 * GROUP
CHUNKS = 2 * SHOTS // GROUP
PER_BATCH = SHOTS // GROUP
COLS = 4 * SHOTS
DOWN, UP = 0, 1
WINDOW = 2
MESH = pl.DeviceIdType.MESH


def column_group(chunk, part):
    return (chunk // PER_BATCH) * 2 * PER_BATCH + part * PER_BATCH + chunk % PER_BATCH


def kernel(
    sections,
    lat_devices,
    operator,
    shift,
    reflect,
    up_stored,
    down_stored,
    sources,
    assignment,
    result,
    raw,
    high,
    low,
    up_rows,
    down_rows,
    source_rows,
    mine,
    local,
    weight,
    terms,
    arrived,
    leaving,
    split,
    load_sem,
    raw_sem,
    term_send,
    term_recv,
    weight_send,
    weight_recv,
    field_send,
    field_recv,
    share_send,
):
    depth = lax.axis_index("depth")
    lat = lax.axis_index("lat")
    tiles = raw.shape[0]
    width = tiles * TILE

    loads = [
        pltpu.make_async_copy(source, target, load_sem.at[n])
        for n, (source, target) in enumerate(
            [
                (sources, source_rows),
                (up_stored.at[0], up_rows),
                (down_stored.at[0], down_rows),
            ]
        )
    ]
    raw_loads = [
        pltpu.make_async_copy(operator.at[0, g], raw.at[g], raw_sem.at[g]) for g in range(tiles)
    ]
    for copy in loads:
        copy.start()
    for copy in raw_loads:
        copy.start()

    def lat_ok(step):
        return (lat + step >= 0) & (lat + step < lat_devices)

    def depth_ok(step):
        return (depth + step >= 0) & (depth + step < sections)

    barrier = pltpu.get_barrier_semaphore()
    greeted = 0
    for down_by in (-1, 0, 1):
        for right_by in (-1, 0, 1):
            if (down_by, right_by) == (0, 0):
                continue
            ok = lat_ok(right_by) & depth_ok(down_by)
            greeted = greeted + ok.astype(jnp.int32)

            @pl.when(ok)
            def _():
                pl.semaphore_signal(
                    barrier,
                    inc=1,
                    device_id=(depth + down_by, lat + right_by),
                    device_id_type=MESH,
                )

    strength = reflect[...]
    mine[...] = jnp.broadcast_to(strength, mine.shape)

    def pieces(rows):
        for g in range(tiles):
            flipped = jnp.transpose(rows[g * TILE : (g + 1) * TILE, :])
            here = slice(g * TILE, (g + 1) * TILE)
            for chunk in range(CHUNKS):
                for part in range(2):
                    group = column_group(chunk, part)
                    place = slice(part * GROUP, (part + 1) * GROUP)
                    yield chunk, place, here, flipped[group * GROUP : (group + 1) * GROUP]

    loads[0].wait()
    loads[1].wait()
    for chunk, place, here, value in pieces(up_rows[...]):
        local[DOWN, chunk, place, here] = -strength[:, here] * value

    @pl.when(depth == 0)
    def _():
        lanes = lax.broadcasted_iota(jnp.int32, (1, COLS), 1)
        wanted = jnp.zeros((1, COLS), jnp.int32)
        for slot in range(2 * SHOTS):
            column = (slot // SHOTS) * 2 * SHOTS + slot % SHOTS
            wanted = jnp.where(lanes == column, assignment[slot], wanted)
            wanted = jnp.where(lanes == column + SHOTS, assignment[slot] + 2 * SHOTS, wanted)
        chosen = (lax.broadcasted_iota(jnp.int32, (COLS, COLS), 0) == wanted).astype(jnp.float32)
        entering = jnp.dot(
            source_rows[...],
            chosen,
            precision=lax.Precision.HIGHEST,
            preferred_element_type=jnp.float32,
        )
        for chunk, place, here, value in pieces(entering):
            arrived[DOWN, chunk, 1, place, here] = (
                local[DOWN, chunk, place, here] + (1.0 + strength[:, here]) * value
            )

    loads[2].wait()
    for chunk, place, here, value in pieces(down_rows[...]):
        local[UP, chunk, place, here] = strength[:, here] * value

    @pl.when(depth == sections - 1)
    def _():
        for chunk in range(CHUNKS):
            arrived[UP, chunk, 1] = local[UP, chunk]

    for edge, slot in ((0, 0), (lat_devices - 1, 2)):

        @pl.when(lat == edge)
        def _():
            def clear(which, _):
                for chunk in range(CHUNKS):
                    arrived[which, chunk, slot] = jnp.zeros((ROWS, width), jnp.float32)
                return 0

            lax.fori_loop(0, 2, clear, 0)

    pl.semaphore_wait(barrier, greeted)

    def term_copy(which, half):
        some = pl.ds(half * (CHUNKS // 2), CHUNKS // 2)
        return pltpu.make_async_remote_copy(
            src_ref=local.at[which, some],
            dst_ref=terms.at[which, some],
            send_sem=term_send.at[which, half],
            recv_sem=term_recv.at[which, half],
            device_id=(depth - 1 + 2 * which, lat),
            device_id_type=MESH,
        )

    def weight_copy(which):
        return pltpu.make_async_remote_copy(
            src_ref=mine,
            dst_ref=weight.at[which],
            send_sem=weight_send.at[which],
            recv_sem=weight_recv.at[which],
            device_id=(depth - 1 + 2 * which, lat),
            device_id_type=MESH,
        )

    def first_copy(which, chunk, step):
        slot = 1 - step
        return pltpu.make_async_remote_copy(
            src_ref=arrived.at[which, chunk, 1],
            dst_ref=arrived.at[which, chunk, slot],
            send_sem=field_send.at[1 - which, chunk, slot],
            recv_sem=field_recv.at[which, chunk, slot],
            device_id=(depth, lat + step),
            device_id_type=MESH,
        )

    def field_copy(which, chunk, step, piece=pl.ds(0, width)):
        slot = 1 - step
        return pltpu.make_async_remote_copy(
            src_ref=leaving.at[which, chunk, :, piece],
            dst_ref=arrived.at[which, chunk, slot, :, piece],
            send_sem=field_send.at[which, chunk, slot],
            recv_sem=field_recv.at[which, chunk, slot],
            device_id=(depth + 1 - 2 * which, lat + step),
            device_id_type=MESH,
        )

    def shares(section):
        return (section < sections // 2 - 1) | (section > sections // 2)

    inner = 1 - 2 * (lat % 2)
    outer = -inner

    def share_copy(which, chunk, arriving=False):
        slot = 1 + inner if arriving else 1 - inner
        return pltpu.make_async_remote_copy(
            src_ref=arrived.at[which, chunk, 1],
            dst_ref=arrived.at[which, chunk, slot],
            send_sem=share_send.at[which, chunk],
            recv_sem=field_recv.at[which, chunk, slot],
            device_id=(depth, lat + inner),
            device_id_type=MESH,
        )

    early = jnp.where(2 * depth < sections, DOWN, UP)
    lag = jnp.where((depth == sections // 2 - 1) | (depth == sections // 2), 3, CHUNKS)

    at_end = (depth == 0) | (depth == sections - 1)

    @pl.when(at_end)
    def _():
        def send_first(chunk, _):
            for step in (-1, 1):

                @pl.when(lat_ok(step))
                def _():
                    first_copy(early, chunk, step).start()

            return 0

        lax.fori_loop(0, 1, send_first, 0)

    for which in (DOWN, UP):

        @pl.when(depth_ok(2 * which - 1))
        def _():
            weight_copy(which).start()

    for half in range(2):
        for which in (DOWN, UP):

            @pl.when(depth_ok(2 * which - 1))
            def _():
                term_copy(which, half).start()

    for copy in raw_loads:
        copy.wait()

    def prepare(g, _):
        for k in range(9):
            flipped = jnp.transpose(raw[g, k])
            lead = flipped.astype(jnp.bfloat16)
            here = slice(k * TILE, (k + 1) * TILE)
            high[g, here, :] = lead
            low[g, here, :] = (flipped - lead.astype(jnp.float32)).astype(jnp.bfloat16)
        return 0

    lax.fori_loop(0, tiles, prepare, 0)

    for which in (DOWN, UP):

        @pl.when(depth_ok(1 - 2 * which))
        def _():
            weight_copy(which).wait_recv()

    split_at = (tiles + 1) // 2

    def process(items):
        count = len(items)
        for which, chunk in items:
            has_in = depth_ok(2 * which - 1)

            @pl.when(has_in)
            def _():
                field_copy(which, chunk, 0).wait_recv()

            @pl.when(has_in & shares(depth))
            def _():
                share_copy(which, chunk).start()

        for n, (which, chunk) in enumerate(items):
            share_copy(which, chunk, arriving=True).wait_recv()

            @pl.when(lat_ok(outer))
            def _():
                field_copy(which, chunk, -outer).wait_recv()

            @pl.when(depth_ok(1 - 2 * which) & (chunk % (CHUNKS // 2) == 0))
            def _():
                term_copy(which, chunk // (CHUNKS // 2)).wait_recv()

            leads = slice(n * ROWS, (n + 1) * ROWS)
            rests = slice((count + n) * ROWS, (count + n + 1) * ROWS)
            for slot in range(3):
                field = arrived[which, chunk, slot]
                lead = field.astype(jnp.bfloat16)
                here = slice(slot * width, (slot + 1) * width)
                split[leads, here] = lead
                split[rests, here] = (field - lead.astype(jnp.float32)).astype(jnp.bfloat16)

        def leave(first, last):
            piece = pl.ds(first * TILE, (last - first) * TILE)
            for which, chunk in items:
                has_out = depth_ok(1 - 2 * which)
                sign = (1 - 2 * which).astype(jnp.float32)

                @pl.when(has_out)
                def _():
                    scale = 1.0 + sign * weight[which, :, piece]
                    scale = jnp.concatenate([scale, scale], axis=0)
                    leaving[which, chunk, :, piece] = (
                        terms[which, chunk, :, piece] + scale * result[which, chunk, :, piece]
                    )

                direct = jnp.logical_not(shares(depth + 1 - 2 * which))
                ways = ((0, True), (inner, direct), (outer, True))
                if first == 0:
                    for step, used in ways:

                        @pl.when(has_out & lat_ok(step) & used & (chunk >= WINDOW))
                        def _():
                            field_copy(which, chunk - WINDOW, step).wait_send()

                for step, used in ways:

                    @pl.when(has_out & lat_ok(step) & used)
                    def _():
                        field_copy(which, chunk, step, piece).start()

        half = count * ROWS
        for g in range(tiles):
            start = (g + 1 + shift[0, g]) * TILE
            window = split[: 2 * half, pl.ds(start, 9 * TILE)]
            both = jnp.dot(window, high[g], preferred_element_type=jnp.float32)
            rest = jnp.dot(window[:half], low[g], preferred_element_type=jnp.float32)
            total = both[:half] + both[half:] + rest
            here = slice(g * TILE, (g + 1) * TILE)
            for n, (which, chunk) in enumerate(items):
                real = total[n * ROWS : n * ROWS + GROUP]
                imag = total[n * ROWS + GROUP : (n + 1) * ROWS]
                result[which, chunk, :GROUP, here] = real[:, :TILE] - imag[:, TILE:]
                result[which, chunk, GROUP:, here] = imag[:, :TILE] + real[:, TILE:]
            if g + 1 in (split_at, tiles):
                leave(0 if g + 1 == split_at else split_at, g + 1)


    def run(number, _):
        @pl.when(at_end & (number + 1 < CHUNKS))
        def _():
            for step in (-1, 1):

                @pl.when(lat_ok(step))
                def _():
                    first_copy(early, number + 1, step).start()

        paired = (number >= lag) & (number < CHUNKS)

        @pl.when(paired)
        def _():
            process([(early, number), (1 - early, number - lag)])

        @pl.when(jnp.logical_not(paired) & (number < CHUNKS + lag))
        def _():
            begun = number < lag
            process([(jnp.where(begun, early, 1 - early), jnp.where(begun, number, number - lag))])

        return 0

    lax.fori_loop(0, 2 * CHUNKS, run, 0)

    for which in (DOWN, UP):

        @pl.when(depth_ok(2 * which - 1))
        def _():
            weight_copy(which).wait_send()
            for half in range(2):
                term_copy(which, half).wait_send()

    @pl.when(at_end)
    def _():
        def finish_first(chunk, _):
            for step in (-1, 1):

                @pl.when(lat_ok(step))
                def _():
                    first_copy(early, chunk, step).wait_send()

            return 0

        lax.fori_loop(0, CHUNKS, finish_first, 0)

    def finish(number, _):
        which, chunk = number // CHUNKS, number % CHUNKS

        @pl.when(depth_ok(2 * which - 1) & shares(depth))
        def _():
            share_copy(which, chunk).wait_send()

        direct = jnp.logical_not(shares(depth + 1 - 2 * which))
        for step, used in ((0, True), (inner, direct), (outer, True)):

            @pl.when(depth_ok(1 - 2 * which) & lat_ok(step) & used & (chunk >= CHUNKS - WINDOW))
            def _():
                field_copy(which, chunk, step).wait_send()

        return 0

    lax.fori_loop(0, 2 * CHUNKS, finish, 0)


def unpack(result, down_out, up_out):
    for which, out in ((DOWN, down_out), (UP, up_out)):
        for g in range(out.shape[0] // TILE):
            here = slice(g * TILE, (g + 1) * TILE)
            groups = [None] * (2 * CHUNKS)
            for chunk in range(CHUNKS):
                for part in range(2):
                    groups[column_group(chunk, part)] = result[
                        which, chunk, part * GROUP : (part + 1) * GROUP, here
                    ]
            out[here, :] = jnp.transpose(jnp.concatenate(groups, axis=0))


def solution(mesh):
    sections = mesh.shape["depth"]
    lat_devices = mesh.shape["lat"]

    def shards(operator, band_shift, reflectivity, up_stored, down_stored, sources, assignment):
        tiles = operator.shape[1]
        width = tiles * TILE
        anywhere = pl.BlockSpec(memory_space=pl.ANY)
        in_vmem = pl.BlockSpec(memory_space=pltpu.VMEM)
        in_smem = pl.BlockSpec(memory_space=pltpu.SMEM)
        dma = pltpu.SemaphoreType.DMA

        def body(*refs):
            kernel(sections, lat_devices, *refs)

        result = pl.pallas_call(
            body,
            out_shape=jax.ShapeDtypeStruct((2, CHUNKS, ROWS, width), jnp.float32),
            in_specs=[anywhere, in_smem, in_vmem, anywhere, anywhere, anywhere, in_smem],
            out_specs=in_vmem,
            scratch_shapes=[
                pltpu.VMEM((tiles, 9, 2 * TILE, TILE), jnp.float32),
                pltpu.VMEM((tiles, 9 * TILE, 2 * TILE), jnp.bfloat16),
                pltpu.VMEM((tiles, 9 * TILE, 2 * TILE), jnp.bfloat16),
                pltpu.VMEM((width, COLS), jnp.float32),
                pltpu.VMEM((width, COLS), jnp.float32),
                pltpu.VMEM((width, COLS), jnp.float32),
                pltpu.VMEM((8, width), jnp.float32),
                pltpu.VMEM((2, CHUNKS, ROWS, width), jnp.float32),
                pltpu.VMEM((2, 8, width), jnp.float32),
                pltpu.VMEM((2, CHUNKS, ROWS, width), jnp.float32),
                pltpu.VMEM((2, CHUNKS, 3, ROWS, width), jnp.float32),
                pltpu.VMEM((2, CHUNKS, ROWS, width), jnp.float32),
                pltpu.VMEM((4 * ROWS, 3 * width), jnp.bfloat16),
                dma((3,)),
                dma((tiles,)),
                dma((2, 2)),
                dma((2, 2)),
                dma((2,)),
                dma((2,)),
                dma((2, CHUNKS, 3)),
                dma((2, CHUNKS, 3)),
                dma((2, CHUNKS)),
            ],
            compiler_params=pltpu.CompilerParams(
                collective_id=0, has_side_effects=True, vmem_limit_bytes=60 * 2**20
            ),
            name="round_trip",
        )(operator, band_shift, reflectivity, up_stored, down_stored, sources, assignment)
        down, up = pl.pallas_call(
            unpack,
            out_shape=[jax.ShapeDtypeStruct((width, COLS), jnp.float32)] * 2,
            in_specs=[in_vmem],
            out_specs=[in_vmem, in_vmem],
            name="unpack",
        )(result)
        return down[None], up[None]

    return jax.shard_map(
        shards,
        mesh=mesh,
        in_specs=(
            P("depth", "lat", None, None, None),
            P("depth", "lat"),
            P("depth", "lat"),
            P("depth", "lat", None),
            P("depth", "lat", None),
            P("lat", None),
            P(),
        ),
        out_specs=(P("depth", "lat", None), P("depth", "lat", None)),
        check_vma=False,
    )
```

```python
import jax
import jax.numpy as jnp
from jax import lax
from jax.experimental import pallas as pl
from jax.experimental.pallas import tpu as pltpu
from jax.sharding import PartitionSpec as P

TILE = 128
SHOTS = 32
GROUP = 8
ROWS = 2 * GROUP
CHUNKS = 2 * SHOTS // GROUP
PER_BATCH = SHOTS // GROUP
COLS = 4 * SHOTS
DOWN, UP = 0, 1
WINDOW = 2
MESH = pl.DeviceIdType.MESH


def column_group(chunk, part):
    return (chunk // PER_BATCH) * 2 * PER_BATCH + part * PER_BATCH + chunk % PER_BATCH


def kernel(
    sections,
    lat_devices,
    operator,
    shift,
    reflect,
    up_stored,
    down_stored,
    sources,
    assignment,
    result,
    raw,
    high,
    low,
    up_rows,
    down_rows,
    source_rows,
    mine,
    local,
    weight,
    terms,
    arrived,
    leaving,
    split,
    load_sem,
    raw_sem,
    term_send,
    term_recv,
    weight_send,
    weight_recv,
    field_send,
    field_recv,
    share_send,
):
    depth = lax.axis_index("depth")
    lat = lax.axis_index("lat")
    tiles = raw.shape[0]
    width = tiles * TILE

    loads = [
        pltpu.make_async_copy(source, target, load_sem.at[n])
        for n, (source, target) in enumerate(
            [
                (sources, source_rows),
                (up_stored.at[0], up_rows),
                (down_stored.at[0], down_rows),
            ]
        )
    ]
    raw_loads = [
        pltpu.make_async_copy(operator.at[0, g], raw.at[g], raw_sem.at[g]) for g in range(tiles)
    ]
    for copy in loads:
        copy.start()
    for copy in raw_loads:
        copy.start()

    def lat_ok(step):
        return (lat + step >= 0) & (lat + step < lat_devices)

    def depth_ok(step):
        return (depth + step >= 0) & (depth + step < sections)

    barrier = pltpu.get_barrier_semaphore()
    greeted = 0
    for down_by in (-1, 0, 1):
        for right_by in (-1, 0, 1):
            if (down_by, right_by) == (0, 0):
                continue
            ok = lat_ok(right_by) & depth_ok(down_by)
            greeted = greeted + ok.astype(jnp.int32)

            @pl.when(ok)
            def _():
                pl.semaphore_signal(
                    barrier,
                    inc=1,
                    device_id=(depth + down_by, lat + right_by),
                    device_id_type=MESH,
                )

    strength = reflect[...]
    mine[...] = jnp.broadcast_to(strength, mine.shape)

    def pieces(rows):
        for g in range(tiles):
            flipped = jnp.transpose(rows[g * TILE : (g + 1) * TILE, :])
            here = slice(g * TILE, (g + 1) * TILE)
            for chunk in range(CHUNKS):
                for part in range(2):
                    group = column_group(chunk, part)
                    place = slice(part * GROUP, (part + 1) * GROUP)
                    yield chunk, place, here, flipped[group * GROUP : (group + 1) * GROUP]

    loads[0].wait()
    loads[1].wait()
    for chunk, place, here, value in pieces(up_rows[...]):
        local[DOWN, chunk, place, here] = -strength[:, here] * value

    @pl.when(depth == 0)
    def _():
        lanes = lax.broadcasted_iota(jnp.int32, (1, COLS), 1)
        wanted = jnp.zeros((1, COLS), jnp.int32)
        for slot in range(2 * SHOTS):
            column = (slot // SHOTS) * 2 * SHOTS + slot % SHOTS
            wanted = jnp.where(lanes == column, assignment[slot], wanted)
            wanted = jnp.where(lanes == column + SHOTS, assignment[slot] + 2 * SHOTS, wanted)
        chosen = (lax.broadcasted_iota(jnp.int32, (COLS, COLS), 0) == wanted).astype(jnp.float32)
        entering = jnp.dot(
            source_rows[...],
            chosen,
            precision=lax.Precision.HIGHEST,
            preferred_element_type=jnp.float32,
        )
        for chunk, place, here, value in pieces(entering):
            arrived[DOWN, chunk, 1, place, here] = (
                local[DOWN, chunk, place, here] + (1.0 + strength[:, here]) * value
            )

    loads[2].wait()
    for chunk, place, here, value in pieces(down_rows[...]):
        local[UP, chunk, place, here] = strength[:, here] * value

    @pl.when(depth == sections - 1)
    def _():
        for chunk in range(CHUNKS):
            arrived[UP, chunk, 1] = local[UP, chunk]

    for edge, slot in ((0, 0), (lat_devices - 1, 2)):

        @pl.when(lat == edge)
        def _():
            def clear(which, _):
                for chunk in range(CHUNKS):
                    arrived[which, chunk, slot] = jnp.zeros((ROWS, width), jnp.float32)
                return 0

            lax.fori_loop(0, 2, clear, 0)

    pl.semaphore_wait(barrier, greeted)

    def term_copy(which, half):
        some = pl.ds(half * (CHUNKS // 2), CHUNKS // 2)
        return pltpu.make_async_remote_copy(
            src_ref=local.at[which, some],
            dst_ref=terms.at[which, some],
            send_sem=term_send.at[which, half],
            recv_sem=term_recv.at[which, half],
            device_id=(depth - 1 + 2 * which, lat),
            device_id_type=MESH,
        )

    def weight_copy(which):
        return pltpu.make_async_remote_copy(
            src_ref=mine,
            dst_ref=weight.at[which],
            send_sem=weight_send.at[which],
            recv_sem=weight_recv.at[which],
            device_id=(depth - 1 + 2 * which, lat),
            device_id_type=MESH,
        )

    def first_copy(which, chunk, step):
        slot = 1 - step
        return pltpu.make_async_remote_copy(
            src_ref=arrived.at[which, chunk, 1],
            dst_ref=arrived.at[which, chunk, slot],
            send_sem=field_send.at[1 - which, chunk, slot],
            recv_sem=field_recv.at[which, chunk, slot],
            device_id=(depth, lat + step),
            device_id_type=MESH,
        )

    def field_copy(which, chunk, step, piece=pl.ds(0, width)):
        slot = 1 - step
        return pltpu.make_async_remote_copy(
            src_ref=leaving.at[which, chunk, :, piece],
            dst_ref=arrived.at[which, chunk, slot, :, piece],
            send_sem=field_send.at[which, chunk, slot],
            recv_sem=field_recv.at[which, chunk, slot],
            device_id=(depth + 1 - 2 * which, lat + step),
            device_id_type=MESH,
        )

    def shares(section):
        return (section < sections // 2 - 1) | (section > sections // 2)

    inner = 1 - 2 * (lat % 2)
    outer = -inner

    def share_copy(which, chunk, arriving=False):
        slot = 1 + inner if arriving else 1 - inner
        return pltpu.make_async_remote_copy(
            src_ref=arrived.at[which, chunk, 1],
            dst_ref=arrived.at[which, chunk, slot],
            send_sem=share_send.at[which, chunk],
            recv_sem=field_recv.at[which, chunk, slot],
            device_id=(depth, lat + inner),
            device_id_type=MESH,
        )

    early = jnp.where(2 * depth < sections, DOWN, UP)
    lag = jnp.where((depth == sections // 2 - 1) | (depth == sections // 2), 3, CHUNKS)

    at_end = (depth == 0) | (depth == sections - 1)

    @pl.when(at_end)
    def _():
        def send_first(chunk, _):
            for step in (-1, 1):

                @pl.when(lat_ok(step))
                def _():
                    first_copy(early, chunk, step).start()

            return 0

        lax.fori_loop(0, 1, send_first, 0)

    for which in (DOWN, UP):

        @pl.when(depth_ok(2 * which - 1))
        def _():
            weight_copy(which).start()

    for half in range(2):
        for which in (DOWN, UP):

            @pl.when(depth_ok(2 * which - 1))
            def _():
                term_copy(which, half).start()

    for copy in raw_loads:
        copy.wait()

    def prepare(g, _):
        for k in range(9):
            flipped = jnp.transpose(raw[g, k])
            lead = flipped.astype(jnp.bfloat16)
            here = slice(k * TILE, (k + 1) * TILE)
            high[g, here, :] = lead
            low[g, here, :] = (flipped - lead.astype(jnp.float32)).astype(jnp.bfloat16)
        return 0

    lax.fori_loop(0, tiles, prepare, 0)

    for which in (DOWN, UP):

        @pl.when(depth_ok(1 - 2 * which))
        def _():
            weight_copy(which).wait_recv()

    split_at = (tiles + 1) // 2

    def process(items):
        count = len(items)
        for which, chunk in items:
            has_in = depth_ok(2 * which - 1)

            @pl.when(has_in)
            def _():
                field_copy(which, chunk, 0).wait_recv()

            @pl.when(has_in & shares(depth))
            def _():
                share_copy(which, chunk).start()

        for n, (which, chunk) in enumerate(items):
            share_copy(which, chunk, arriving=True).wait_recv()

            @pl.when(lat_ok(outer))
            def _():
                field_copy(which, chunk, -outer).wait_recv()

            @pl.when(depth_ok(1 - 2 * which) & (chunk % (CHUNKS // 2) == 0))
            def _():
                term_copy(which, chunk // (CHUNKS // 2)).wait_recv()

            leads = slice(n * ROWS, (n + 1) * ROWS)
            rests = slice((count + n) * ROWS, (count + n + 1) * ROWS)
            for slot in range(3):
                field = arrived[which, chunk, slot]
                lead = field.astype(jnp.bfloat16)
                here = slice(slot * width, (slot + 1) * width)
                split[leads, here] = lead
                split[rests, here] = (field - lead.astype(jnp.float32)).astype(jnp.bfloat16)

        def leave(first, last):
            piece = pl.ds(first * TILE, (last - first) * TILE)
            for which, chunk in items:
                has_out = depth_ok(1 - 2 * which)
                sign = (1 - 2 * which).astype(jnp.float32)

                @pl.when(has_out)
                def _():
                    scale = 1.0 + sign * weight[which, :, piece]
                    scale = jnp.concatenate([scale, scale], axis=0)
                    leaving[which, chunk, :, piece] = (
                        terms[which, chunk, :, piece] + scale * result[which, chunk, :, piece]
                    )

                direct = jnp.logical_not(shares(depth + 1 - 2 * which))
                ways = ((0, True), (inner, direct), (outer, True))
                if first == 0:
                    for step, used in ways:

                        @pl.when(has_out & lat_ok(step) & used & (chunk >= WINDOW))
                        def _():
                            field_copy(which, chunk - WINDOW, step).wait_send()

                for step, used in ways:

                    @pl.when(has_out & lat_ok(step) & used)
                    def _():
                        field_copy(which, chunk, step, piece).start()

        half = count * ROWS
        for g in range(tiles):
            start = (g + 1 + shift[0, g]) * TILE
            window = split[: 2 * half, pl.ds(start, 9 * TILE)]
            both = jnp.dot(window, high[g], preferred_element_type=jnp.float32)
            rest = jnp.dot(window[:half], low[g], preferred_element_type=jnp.float32)
            total = both[:half] + both[half:] + rest
            here = slice(g * TILE, (g + 1) * TILE)
            for n, (which, chunk) in enumerate(items):
                real = total[n * ROWS : n * ROWS + GROUP]
                imag = total[n * ROWS + GROUP : (n + 1) * ROWS]
                result[which, chunk, :GROUP, here] = real[:, :TILE] - imag[:, TILE:]
                result[which, chunk, GROUP:, here] = imag[:, :TILE] + real[:, TILE:]
            if g + 1 in (split_at, tiles):
                leave(0 if g + 1 == split_at else split_at, g + 1)


    def run(number, _):
        @pl.when(at_end & (number + 1 < CHUNKS))
        def _():
            for step in (-1, 1):

                @pl.when(lat_ok(step))
                def _():
                    first_copy(early, number + 1, step).start()

        paired = (number >= lag) & (number < CHUNKS)

        @pl.when(paired)
        def _():
            process([(early, number), (1 - early, number - lag)])

        @pl.when(jnp.logical_not(paired) & (number < CHUNKS + lag))
        def _():
            begun = number < lag
            process([(jnp.where(begun, early, 1 - early), jnp.where(begun, number, number - lag))])

        return 0

    lax.fori_loop(0, 2 * CHUNKS, run, 0)

    for which in (DOWN, UP):

        @pl.when(depth_ok(2 * which - 1))
        def _():
            weight_copy(which).wait_send()
            for half in range(2):
                term_copy(which, half).wait_send()

    @pl.when(at_end)
    def _():
        def finish_first(chunk, _):
            for step in (-1, 1):

                @pl.when(lat_ok(step))
                def _():
                    first_copy(early, chunk, step).wait_send()

            return 0

        lax.fori_loop(0, CHUNKS, finish_first, 0)

    def finish(number, _):
        which, chunk = number // CHUNKS, number % CHUNKS

        @pl.when(depth_ok(2 * which - 1) & shares(depth))
        def _():
            share_copy(which, chunk).wait_send()

        direct = jnp.logical_not(shares(depth + 1 - 2 * which))
        for step, used in ((0, True), (inner, direct), (outer, True)):

            @pl.when(depth_ok(1 - 2 * which) & lat_ok(step) & used & (chunk >= CHUNKS - WINDOW))
            def _():
                field_copy(which, chunk, step).wait_send()

        return 0

    lax.fori_loop(0, 2 * CHUNKS, finish, 0)


def unpack(result, down_out, up_out, held, turned, in_sem, out_sem):
    outs = (down_out, up_out)
    tiles = down_out.shape[0] // TILE

    def load(which, g):
        here = pl.ds(g * TILE, TILE)
        return pltpu.make_async_copy(
            result.at[which, :, :, here], held.at[which, :, :, here], in_sem.at[which, g]
        )

    def store(which, g):
        here = pl.ds(g * TILE, TILE)
        return pltpu.make_async_copy(
            turned.at[which, here], outs[which].at[here], out_sem.at[which, g]
        )

    order = [(which, g) for which in (DOWN, UP) for g in range(tiles)]
    for which, g in order:
        load(which, g).start()
    for which, g in order:
        load(which, g).wait()
        here = slice(g * TILE, (g + 1) * TILE)
        groups = [None] * (2 * CHUNKS)
        for chunk in range(CHUNKS):
            for part in range(2):
                groups[column_group(chunk, part)] = held[
                    which, chunk, part * GROUP : (part + 1) * GROUP, here
                ]
        turned[which, here, :] = jnp.transpose(jnp.concatenate(groups, axis=0))
        store(which, g).start()
    for which, g in order:
        store(which, g).wait()


def solution(mesh):
    sections = mesh.shape["depth"]
    lat_devices = mesh.shape["lat"]

    def shards(operator, band_shift, reflectivity, up_stored, down_stored, sources, assignment):
        tiles = operator.shape[1]
        width = tiles * TILE
        anywhere = pl.BlockSpec(memory_space=pl.ANY)
        in_vmem = pl.BlockSpec(memory_space=pltpu.VMEM)
        in_smem = pl.BlockSpec(memory_space=pltpu.SMEM)
        dma = pltpu.SemaphoreType.DMA

        def body(*refs):
            kernel(sections, lat_devices, *refs)

        result = pl.pallas_call(
            body,
            out_shape=jax.ShapeDtypeStruct((2, CHUNKS, ROWS, width), jnp.float32),
            in_specs=[anywhere, in_smem, in_vmem, anywhere, anywhere, anywhere, in_smem],
            out_specs=in_vmem,
            scratch_shapes=[
                pltpu.VMEM((tiles, 9, 2 * TILE, TILE), jnp.float32),
                pltpu.VMEM((tiles, 9 * TILE, 2 * TILE), jnp.bfloat16),
                pltpu.VMEM((tiles, 9 * TILE, 2 * TILE), jnp.bfloat16),
                pltpu.VMEM((width, COLS), jnp.float32),
                pltpu.VMEM((width, COLS), jnp.float32),
                pltpu.VMEM((width, COLS), jnp.float32),
                pltpu.VMEM((8, width), jnp.float32),
                pltpu.VMEM((2, CHUNKS, ROWS, width), jnp.float32),
                pltpu.VMEM((2, 8, width), jnp.float32),
                pltpu.VMEM((2, CHUNKS, ROWS, width), jnp.float32),
                pltpu.VMEM((2, CHUNKS, 3, ROWS, width), jnp.float32),
                pltpu.VMEM((2, CHUNKS, ROWS, width), jnp.float32),
                pltpu.VMEM((4 * ROWS, 3 * width), jnp.bfloat16),
                dma((3,)),
                dma((tiles,)),
                dma((2, 2)),
                dma((2, 2)),
                dma((2,)),
                dma((2,)),
                dma((2, CHUNKS, 3)),
                dma((2, CHUNKS, 3)),
                dma((2, CHUNKS)),
            ],
            compiler_params=pltpu.CompilerParams(
                collective_id=0, has_side_effects=True, vmem_limit_bytes=60 * 2**20
            ),
            name="round_trip",
        )(operator, band_shift, reflectivity, up_stored, down_stored, sources, assignment)
        down, up = pl.pallas_call(
            unpack,
            out_shape=[jax.ShapeDtypeStruct((width, COLS), jnp.float32)] * 2,
            in_specs=[anywhere],
            out_specs=[anywhere, anywhere],
            scratch_shapes=[
                pltpu.VMEM((2, CHUNKS, ROWS, width), jnp.float32),
                pltpu.VMEM((2, width, COLS), jnp.float32),
                dma((2, tiles)),
                dma((2, tiles)),
            ],
            compiler_params=pltpu.CompilerParams(vmem_limit_bytes=60 * 2**20),
            name="unpack",
        )(result)
        return down[None], up[None]

    return jax.shard_map(
        shards,
        mesh=mesh,
        in_specs=(
            P("depth", "lat", None, None, None),
            P("depth", "lat"),
            P("depth", "lat"),
            P("depth", "lat", None),
            P("depth", "lat", None),
            P("lat", None),
            P(),
        ),
        out_specs=(P("depth", "lat", None), P("depth", "lat", None)),
        check_vma=False,
    )
```
